256 devices in a mesh: ctx: 32 (over z, y), head: 8 (over x, core).
Axes of the slice: x: 4, y: 4, z: 8, core: 2. Of those that a mesh axis runs over, the one named last changes fastest.
Arguments:
- queries: bfloat16 [32768, 4096], P('ctx', 'head'), may hold values from -110 to 110
- keys: bfloat16 [32768, 1024], P('ctx', 'head'), may hold values from -4 to 4
- values: bfloat16 [32768, 1024], P('ctx', 'head'), may hold values from -6 to 6
- pairs: int32 [256, 8], P('ctx'), may hold values from -1 to 255, as said below
- positions: int32 [1024], replicated, may hold values from 0 to 32767, as said below
- w_out: bfloat16 [4096, 4096], P('head', 'ctx'), may hold values from -0.09375 to 0.09375
Outputs:
- mixed: bfloat16 [32768, 4096], P(('ctx', 'head'))
The draws below stay inside these ranges and needn't reach their ends.
Inputs may be any that keep to these rules, and one draw needn't show every extreme that they name: `pairs`: entry l of query block b is either b XOR 2^l or -1, and is -1 whenever 2^l >= 256. `positions`: distinct and ascending; exactly 32 of them lie in each index of ctx's 1024 tokens.
All inputs are finite; a program needn't handle non-finite values.
Results may differ from the reference program's by a relative error of at most 0.0057.
Values may be sent and summed in bfloat16 or wider, within the bound.
A program may use at most 64 MiB of HBM per device.

```python
import math
import jax
import jax.numpy as jnp
from jax import lax

D = 4096
HEADS = 32
KVH = 8
HD = 128
BLK = 128
LEVELS = 8
G = 1024
TOK_DEV = 1024
TOKENS = 32768
N_CTX = 32


def global_spots(key):
    key = jax.random.fold_in(key, 11)
    per_device = G // N_CTX
    device_keys = jax.random.split(key, N_CTX)
    picks = jax.vmap(lambda single: jax.random.permutation(single, TOK_DEV)[:per_device])(device_keys)
    picks = jnp.sort(picks, axis=1) + (jnp.arange(N_CTX, dtype=jnp.int32) * TOK_DEV)[:, None]
    return picks.reshape(G).astype(jnp.int32)


def key_field(key):
    spots = global_spots(key)
    base = jnp.clip(jax.random.normal(jax.random.fold_in(key, 5), (TOKENS, KVH * HD), jnp.float32), -4.0, 4.0)
    followers = spots[1::16]
    base = base.at[followers].set(base[followers])
    return base


def draw_keys(key, part):
    return key_field(key).astype(jnp.bfloat16)


def draw_queries(key, part):
    key = jax.random.fold_in(key, 7)
    drawn = jnp.clip(jax.random.normal(key, (TOKENS, HEADS * HD), jnp.float32), -4.0, 4.0)
    return drawn.astype(jnp.bfloat16)


def draw_positions(key, part):
    return global_spots(key)


def draw_pairs(key, part):
    key = jax.random.fold_in(key, 3)
    blocks = TOKENS // BLK
    per_device = TOK_DEV // BLK
    first, second = jax.random.split(key)
    density = jax.random.randint(first, (N_CTX,), 1, 5)
    roll = jax.random.randint(second, (blocks, LEVELS), 0, 4)
    block = jnp.arange(blocks, dtype=jnp.int32)
    level = jnp.arange(LEVELS, dtype=jnp.int32)
    span = jnp.left_shift(jnp.int32(1), level)
    keep = (roll < density[block // per_device][:, None]) & (span[None, :] < blocks)
    forced_on = (block[:, None] == blocks // 2 - 1) & (span[None, :] == blocks // 2)
    forced_off = (block[:, None] == blocks - 1) & (level[None, :] == 0)
    keep = (keep | forced_on) & jnp.logical_not(forced_off)
    partner = jnp.bitwise_xor(block[:, None], span[None, :])
    return jnp.where(keep, partner, -1).astype(jnp.int32)


def block_levels(rng, shape, pieces, least, top_value):
    def one(dim, parts):
        steps = jax.random.uniform(jax.random.fold_in(jax.random.fold_in(rng, 6), dim), (parts,), jnp.float32, least / len(pieces), top_value / len(pieces))
        return jnp.repeat(jnp.exp(steps), shape[dim] // parts).reshape((-1,) + (1,) * (len(shape) - dim - 1))

    gain = one(*pieces[0])
    for cut in pieces[1:]:
        gain = gain * one(*cut)
    return gain


def noise(stream_key, extent, deviation, reach, cuts=(), held_as=jnp.bfloat16):
    array = jax.random.normal(stream_key, extent, jnp.float32) * deviation
    if len(cuts) > 0:
        array = block_levels(stream_key, extent, cuts, -0.22, 0.18) * array
    return jnp.clip(array, min=-reach, max=reach).astype(held_as)


def setup_inputs(seed: int = 0) -> dict:
    seeds = jax.random.split(jax.random.key(seed), 7)
    queries = draw_queries(jax.random.fold_in(seeds[6], 71), 0)
    keys = draw_keys(jax.random.fold_in(seeds[6], 71), 0)
    values = noise(seeds[2], (TOKENS, KVH * HD), 1.0, 6.0, ((0, 32), (1, 8)))
    pairs = draw_pairs(jax.random.fold_in(seeds[6], 71), 0)
    positions = draw_positions(jax.random.fold_in(seeds[6], 71), 0)
    w_out = noise(seeds[5], (HEADS * HD, D), (HEADS * HD) ** -0.5, 0.09375, ((0, 8), (1, 32)))
    return dict(queries=queries, keys=keys, values=values, pairs=pairs, positions=positions, w_out=w_out)


def reference(queries, keys, values, pairs, positions, w_out):
    groups = HEADS // KVH
    blocks = TOKENS // BLK
    query_blocks = queries.reshape(blocks, BLK, KVH, groups, HD)
    key_blocks = keys.reshape(blocks, BLK, KVH, HD)
    value_blocks = values.reshape(blocks, BLK, KVH, HD)
    global_keys = keys[positions].reshape(G, KVH, HD)
    global_values = values[positions].reshape(G, KVH, HD)
    scale = 1.0 / math.sqrt(HD)

    def one_block(index):
        row = pairs[index]
        valid = row >= 0
        chosen = jnp.where(valid, row, index).astype(jnp.int32)
        key_set = jnp.concatenate([key_blocks[index], key_blocks[chosen].reshape(LEVELS * BLK, KVH, HD), global_keys], axis=0)
        value_set = jnp.concatenate([value_blocks[index], value_blocks[chosen].reshape(LEVELS * BLK, KVH, HD), global_values], axis=0)
        visible = jnp.concatenate([jnp.ones((BLK,), jnp.bool_), jnp.repeat(valid, BLK), jnp.ones((G,), jnp.bool_)])
        scores = jnp.einsum('qkgd,nkd->qkgn', query_blocks[index].astype(jnp.float32), key_set.astype(jnp.float32)) * scale
        scores = jnp.where(visible, scores, -jnp.inf)
        top = lax.optimization_barrier(jnp.max(scores, axis=-1, keepdims=True))
        weights = jnp.exp(scores - top)
        total = lax.optimization_barrier(jnp.sum(weights, axis=-1, keepdims=True))
        rounded = lax.optimization_barrier(weights.astype(jnp.bfloat16))
        attended = jnp.einsum('qkgn,nkd->qkgd', rounded.astype(jnp.float32), value_set.astype(jnp.float32)) / total
        attended = attended.astype(jnp.bfloat16).reshape(BLK, HEADS * HD)
        return jnp.dot(attended, w_out, preferred_element_type=jnp.float32).astype(jnp.bfloat16)
    mixed = lax.map(one_block, jnp.arange(blocks, dtype=jnp.int32))
    return mixed.reshape(TOKENS, D)
```

```python
import math

import jax
import jax.numpy as jnp
from jax import lax
from jax.experimental import pallas as pl
from jax.experimental.pallas import tpu as pltpu
from jax.sharding import PartitionSpec as P

HD = 128
BLK = 128
BLOCKS = 8
CHUNKS = 4
ROWS = 2 * BLK
GROUPS = 4
NY, NZ, NX = 4, 8, 4
PICK = 32
KEYS = 9 * BLK + NY * NZ * PICK
SCALE = math.log2(math.e) / math.sqrt(HD)
MESH = pl.DeviceIdType.MESH
ORDER = (2, 1, 3, 0)


def flip(value, span):
    return value + span - 2 * span * ((value // span) % 2)


def kernel(
    q_hbm, k_hbm, v_hbm, pairs_ref, pos_ref, w_hbm, out_ref,
    q_ref, kv_own, kv_in, g_ref, w_own, w_sib, s_ref, p_ref, att_ref, att_in,
    p_send, r1a, r1b, r2a, r2b, acc_ref,
    load_sem, kv_ssem, kv_rsem, g_ssem, g_rsem, zu_s, zu_r, zd_s, zd_r,
    yu_s, yu_r, yd_s, yd_r, far_s, far_r, sib_s, sib_r, att_s, att_r,
    one_s, one_r, two_s, two_r,
):
    ctx = lax.axis_index("ctx")
    head = lax.axis_index("head")
    z, y = ctx // NY, ctx % NY
    x, core = head // 2, head % 2

    def at(zz, yy):
        return (zz * NY + yy, head)

    z_up, z_dn = (z + 1) % NZ, (z + NZ - 1) % NZ
    y_up, y_dn, y_far = (y + 1) % NY, (y + NY - 1) % NY, (y + 2) % NY
    zu, zd, yu, yd, yf = at(z_up, y), at(z_dn, y), at(z, y_up), at(z, y_dn), at(z, y_far)
    sibling = (ctx, flip(head, 1))
    xu = (ctx, ((x + 1) % NX) * 2 + core)
    xd = (ctx, ((x + NX - 1) % NX) * 2 + core)
    partners = (at(z, flip(y, 1)), yf, at(flip(z, 1), y), at(flip(z, 2), y), at((z + 4) % NZ, y))

    loads = [
        pltpu.make_async_copy(w_hbm, w_own.at[y, z], load_sem.at[0]),
        pltpu.make_async_copy(k_hbm, kv_own.at[:, 0], load_sem.at[1]),
        pltpu.make_async_copy(v_hbm, kv_own.at[:, 1], load_sem.at[2]),
        pltpu.make_async_copy(q_hbm, q_ref, load_sem.at[3]),
    ]
    for load in loads:
        load.start()

    barrier = pltpu.get_barrier_semaphore()
    peers = (zu, zd, yu, yd, yf, partners[3], partners[4], sibling, xu, xd)
    for peer in peers:
        pl.semaphore_signal(barrier, inc=1, device_id=peer, device_id_type=MESH)
    pl.semaphore_wait(barrier, len(peers))

    sent = []

    def send(src, dst, ssem, rsem, device):
        copy = pltpu.make_async_remote_copy(
            src_ref=src, dst_ref=dst, send_sem=ssem, recv_sem=rsem,
            device_id=device, device_id_type=MESH,
        )
        copy.start()
        sent.append(copy)

    def arrived(dst, rsem):
        pltpu.make_async_copy(dst, dst, rsem).wait()

    slots = [z, z_dn, z_up, (z + 6) % NZ, (z + 2) % NZ, (z + 5) % NZ, (z + 3) % NZ, (z + 4) % NZ]

    def spread(e):
        ref = w_own.at[y, slots[e]]
        send(ref, ref, yu_s.at[e], yu_r.at[e], yu)
        send(ref, ref, yd_s.at[e], yd_r.at[e], yd)

    def z_step(t):
        if t > 0:
            arrived(w_own.at[y, slots[2 * t - 1]], zu_r.at[t - 1])
        if t < 4:
            ref = w_own.at[y, z if t == 0 else slots[2 * t - 1]]
            send(ref, ref, zu_s.at[t], zu_r.at[t], zu)
        if 0 < t < 4:
            arrived(w_own.at[y, slots[2 * t]], zd_r.at[t - 1])
        if t < 3:
            ref = w_own.at[y, slots[2 * t]]
            send(ref, ref, zd_s.at[t], zd_r.at[t], zd)
        if t == 0:
            spread(0)
        else:
            spread(2 * t - 1)
            if t < 4:
                spread(2 * t)

    def y_step(e):
        low, high = w_own.at[y_dn, slots[e]], w_own.at[y_up, slots[e]]
        arrived(low, yu_r.at[e])
        if e % 2 == 0:
            send(low, low, far_s.at[e], far_r.at[e], yu)
        arrived(high, yd_r.at[e])
        if e % 2 == 1:
            send(high, high, far_s.at[e], far_r.at[e], yd)

    def share(n, yy):
        send(w_own.at[yy], w_sib.at[yy], sib_s.at[n], sib_r.at[n], sibling)

    def kv_send(s):
        i = (x + ORDER[s]) % NX
        for n in (4, 3, 2, 1, 0):
            send(kv_own.at[i], kv_in.at[n, i], kv_ssem.at[n, s], kv_rsem.at[n, s], partners[n])

    loads[0].wait()
    z_step(0)
    loads[1].wait()
    loads[2].wait()
    kv_send(0)

    wanted = pos_ref[pl.ds(ctx, 1), :]
    zpos = z // 4 + 2 * ((z // 2) % 2) + 4 * (z % 2)
    for part in range(2):
        picked = jnp.zeros((PICK, HD), jnp.float32)
        for i in range(CHUNKS):
            spot = lax.broadcasted_iota(jnp.int32, (ROWS, PICK), 0) + (ctx * 1024 + i * ROWS)
            chosen = (spot == wanted).astype(jnp.float32).astype(jnp.bfloat16)
            picked += lax.dot_general(
                chosen, kv_own[i, part], (((0,), (0,)), ((), ())),
                preferred_element_type=jnp.float32,
            )
        g_ref[part, y, pl.ds(pl.multiple_of(zpos * PICK, PICK), PICK), :] = picked.astype(jnp.bfloat16)

    def g_rows(yy, size, slot):
        start = (slot // size) * size * PICK
        return g_ref.at[:, yy, pl.ds(pl.multiple_of(start, size * PICK), size * PICK), :]

    for n, partner in enumerate((partners[4], partners[3], partners[2])):
        size = 1 << n
        mine = g_rows(y, size, zpos)
        send(mine, mine, g_ssem.at[n], g_rsem.at[n], partner)
        arrived(g_rows(y, size, flip(zpos, size)), g_rsem.at[n])
        if n < 2:
            z_step(n + 1)
    whole = g_ref.at[:, y]
    for n, peer in enumerate((yu, yd, yf)):
        send(whole, whole, g_ssem.at[3 + n], g_rsem.at[3 + n], peer)
    kv_send(1)
    z_step(3)
    for n, yy in enumerate((y_dn, y_up, y_far)):
        arrived(g_ref.at[:, yy], g_rsem.at[3 + n])
    loads[3].wait()

    def attend(i, t):
        j = 2 * i + t
        own = [j, flip(j, 1), flip(j, 2), flip(j, 4)]

        def block(part, n):
            if n < 4:
                jj = own[n]
                return kv_own[jj // 2, part, pl.ds(pl.multiple_of((jj % 2) * BLK, BLK), BLK), :]
            return kv_in[n - 4, i, part, pl.ds(t * BLK, BLK), :]

        rows = pl.ds(pl.multiple_of(j * BLK, BLK), BLK)
        queries = jnp.concatenate(
            [q_ref[rows, h * HD : (h + 1) * HD] for h in range(GROUPS)], axis=0
        )
        contract = (((1,), (1,)), ((), ()))

        def bias(n):
            return jnp.where(pairs_ref[j, n - 1] >= 0, 0.0, -jnp.inf).astype(jnp.float32)

        for first in range(0, 9, 2):
            names = list(range(first, min(first + 2, 9)))
            keys = jnp.concatenate([block(0, n) for n in names], axis=0)
            scores = lax.dot_general(queries, keys, contract, preferred_element_type=jnp.float32)
            for m, n in enumerate(names):
                part = scores[:, m * BLK : (m + 1) * BLK]
                if n > 0:
                    part = part + bias(n)
                s_ref[:, n * BLK : (n + 1) * BLK] = part
        for yy in range(NY):
            start = 9 * BLK + yy * NZ * PICK
            s_ref[:, start : start + NZ * PICK] = lax.dot_general(
                queries, g_ref[0, yy], contract, preferred_element_type=jnp.float32
            )
        totals = []
        for r in range(0, GROUPS * BLK, 64):
            scores = s_ref[r : r + 64, :]
            top = jnp.max(scores, axis=1, keepdims=True)
            weights = jnp.exp2((scores - top) * SCALE)
            totals.append(jnp.sum(weights, axis=1, keepdims=True))
            p_ref[r : r + 64, :] = weights.astype(jnp.bfloat16)
        values = jnp.concatenate(
            [block(1, n) for n in range(9)] + [g_ref[1, yy] for yy in range(NY)], axis=0
        )
        result = jnp.dot(p_ref[...], values, preferred_element_type=jnp.float32)
        result = (result / jnp.concatenate(totals, axis=0)).astype(jnp.bfloat16)
        for h in range(GROUPS):
            att_ref[i, t, :, h * HD : (h + 1) * HD] = result[h * BLK : (h + 1) * BLK]

    for s in range(CHUNKS):
        i = (x + ORDER[s]) % NX
        for n in range(5):
            arrived(kv_in.at[n, i], kv_rsem.at[n, s])
        for t in range(2):
            attend(i, t)
        send(att_ref.at[i, 1 - core], att_in.at[i], att_s.at[s], att_r.at[s], sibling)
        if s == 0:
            kv_send(2)
            z_step(4)
            share(0, y)
            for e in range(4):
                y_step(e)
        if s == 1:
            kv_send(3)
            for e in range(4, 8):
                y_step(e)
            share(1, y_dn)
            share(2, y_up)
        if s == 2:
            for e in range(8):
                arrived(w_own.at[y_far, slots[e]], far_r.at[e])
            share(3, y_far)

    for n, yy in enumerate((y, y_up, y_dn, y_far)):
        arrived(w_sib.at[yy], sib_r.at[(0, 2, 1, 3)[n]])

    def project(i, q, extra, put):
        left, right = att_ref[i, core], att_in[i]
        for half in range(4):
            zz, yy = 2 * q + half // 2, 2 * (half % 2)
            columns = slice(half * 256, half * 256 + 256)
            total = jnp.dot(
                left, jnp.concatenate([w_own[yy, zz], w_own[yy + 1, zz]], axis=1),
                preferred_element_type=jnp.float32,
            ) + jnp.dot(
                right, jnp.concatenate([w_sib[yy, zz], w_sib[yy + 1, zz]], axis=1),
                preferred_element_type=jnp.float32,
            )
            if extra is not None:
                total = total + extra[:, columns].astype(jnp.float32)
            put(columns, total)

    def project_send(n, i, q, extra, dst, ssem, rsem, device):
        def put(columns, total):
            p_send[n, q, :, columns] = total.astype(jnp.bfloat16)

        project(i, q, extra, put)
        send(p_send.at[n, q], dst, ssem, rsem, device)

    for s in range(CHUNKS):
        i = (x + ORDER[s]) % NX
        arrived(att_in.at[i], att_r.at[s])
    far, up, down = (x + 2) % NX, (x + 1) % NX, (x + 3) % NX
    for q in (0, 2, 1, 3):
        dst, device = (r1a.at[q], xu) if q < 2 else (r1b.at[q - 2], xd)
        project_send(0, far, q, None, dst, one_s.at[q], one_r.at[q], device)
    for q in (2, 3):
        project_send(1, up, q, None, r2a.at[q], two_s.at[q], two_r.at[q], xu)
        project_send(2, down, q - 2, None, r2b.at[q - 2], two_s.at[q + 2], two_r.at[q + 2], xd)
    for q in (0, 1):
        arrived(r1a.at[q], one_r.at[q])
        project_send(1, up, q, r1a.at[q], r2a.at[q], two_s.at[q], two_r.at[q], xu)
        arrived(r1b.at[q], one_r.at[q + 2])
        project_send(2, down, q + 2, r1b.at[q], r2b.at[q + 2], two_s.at[q + 6], two_r.at[q + 6], xd)

    for q in range(4):

        def put(columns, total, q=q):
            acc_ref[q, :, columns] = total

        project(x, q, None, put)
    for q in (2, 0, 3, 1):
        arrived(r2a.at[q], two_r.at[q])
        arrived(r2b.at[q], two_r.at[q + 4])
        out_ref[:, q * 1024 : q * 1024 + 1024] = (
            acc_ref[q] + r2a[q].astype(jnp.float32) + r2b[q].astype(jnp.float32)
        ).astype(jnp.bfloat16)
    for copy in sent:
        copy.wait_send()


def shards(queries, keys, values, pairs, positions, w_out):
    bf16, f32 = jnp.bfloat16, jnp.float32
    dma = pltpu.SemaphoreType.DMA
    hbm = pl.BlockSpec(memory_space=pl.ANY)
    return pl.pallas_call(
        kernel,
        out_shape=jax.ShapeDtypeStruct((BLK, 4096), bf16),
        in_specs=[
            hbm, hbm, hbm,
            pl.BlockSpec(memory_space=pltpu.SMEM),
            pl.BlockSpec(memory_space=pltpu.VMEM),
            hbm,
        ],
        out_specs=pl.BlockSpec(memory_space=pltpu.VMEM),
        scratch_shapes=[
            pltpu.VMEM((1024, GROUPS * HD), bf16),
            pltpu.VMEM((CHUNKS, 2, ROWS, HD), bf16),
            pltpu.VMEM((5, CHUNKS, 2, ROWS, HD), bf16),
            pltpu.VMEM((2, NY, NZ * PICK, HD), bf16),
            pltpu.VMEM((NY, NZ, 512, HD), bf16),
            pltpu.VMEM((NY, NZ, 512, HD), bf16),
            pltpu.VMEM((GROUPS * BLK, KEYS), f32),
            pltpu.VMEM((GROUPS * BLK, KEYS), bf16),
            pltpu.VMEM((CHUNKS, 2, BLK, GROUPS * HD), bf16),
            pltpu.VMEM((CHUNKS, BLK, GROUPS * HD), bf16),
            pltpu.VMEM((3, 4, BLK, 1024), bf16),
            pltpu.VMEM((2, BLK, 1024), bf16),
            pltpu.VMEM((2, BLK, 1024), bf16),
            pltpu.VMEM((4, BLK, 1024), bf16),
            pltpu.VMEM((4, BLK, 1024), bf16),
            pltpu.VMEM((4, BLK, 1024), f32),
            dma((4,)), dma((5, CHUNKS)), dma((5, CHUNKS)), dma((6,)), dma((6,)),
            dma((4,)), dma((4,)), dma((3,)), dma((3,)),
            dma((8,)), dma((8,)), dma((8,)), dma((8,)), dma((8,)), dma((8,)),
            dma((4,)), dma((4,)), dma((4,)), dma((4,)),
            dma((4,)), dma((4,)), dma((8,)), dma((8,)),
        ],
        compiler_params=pltpu.CompilerParams(
            collective_id=0, has_side_effects=True, vmem_limit_bytes=56 * 2**20
        ),
        name="butterfly",
    )(
        queries,
        keys.reshape(CHUNKS, ROWS, HD),
        values.reshape(CHUNKS, ROWS, HD),
        pairs,
        positions.reshape(NY * NZ, PICK),
        w_out,
    )


def solution(mesh):
    return jax.shard_map(
        shards,
        mesh=mesh,
        in_specs=(
            P("ctx", "head"),
            P("ctx", "head"),
            P("ctx", "head"),
            P("ctx", None),
            P(),
            P("head", "ctx"),
        ),
        out_specs=P(("ctx", "head"), None),
        check_vma=False,
    )
```

```python
import math

import jax
import jax.numpy as jnp
from jax import lax
from jax.experimental import pallas as pl
from jax.experimental.pallas import tpu as pltpu
from jax.sharding import PartitionSpec as P

HD = 128
BLK = 128
BLOCKS = 8
CHUNKS = 4
ROWS = 2 * BLK
GROUPS = 4
NY, NZ, NX = 4, 8, 4
PICK = 32
KEYS = 9 * BLK + NY * NZ * PICK
SCALE = math.log2(math.e) / math.sqrt(HD)
MESH = pl.DeviceIdType.MESH
ORDER = (2, 1, 3, 0)


def flip(value, span):
    return value + span - 2 * span * ((value // span) % 2)


def kernel(
    q_hbm, k_hbm, v_hbm, pairs_ref, pos_ref, w_hbm, out_ref,
    q_ref, kv_own, kv_in, g_ref, w_own, w_sib, s_ref, p_ref, att_ref, att_in,
    p_send, r1a, r1b, r2a, r2b, acc_ref, pick_ref,
    load_sem, kv_s, kv_r, g_ssem, g_rsem, zu_s, zu_r, zd_s, zd_r,
    yu_s, yu_r, yd_s, yd_r, far_s, far_r, sib_s, sib_r, att_s, att_r,
    one_s, one_r, two_s, two_r,
):
    ctx = lax.axis_index("ctx")
    head = lax.axis_index("head")
    z, y = ctx // NY, ctx % NY
    x, core = head // 2, head % 2

    def at(zz, yy):
        return (zz * NY + yy, head)

    z_up, z_dn = (z + 1) % NZ, (z + NZ - 1) % NZ
    y_up, y_dn, y_far = (y + 1) % NY, (y + NY - 1) % NY, (y + 2) % NY
    zu, zd, yu, yd, yf = at(z_up, y), at(z_dn, y), at(z, y_up), at(z, y_dn), at(z, y_far)
    sibling = (ctx, flip(head, 1))
    xu = (ctx, ((x + 1) % NX) * 2 + core)
    xd = (ctx, ((x + NX - 1) % NX) * 2 + core)
    z_far = (z + 4) % NZ
    z1, z2, z4 = at(flip(z, 1), y), at(flip(z, 2), y), at(z_far, y)
    z3, z6 = at(flip(flip(z, 1), 2), y), at(flip(z_far, 2), y)
    y1, y3 = at(z, flip(y, 1)), at(z, flip((y + 2) % NY, 1))
    inner = ((z + 1) // 2) % 2 == 1

    loads = [
        pltpu.make_async_copy(w_hbm, w_own.at[y, z], load_sem.at[0]),
        pltpu.make_async_copy(k_hbm, kv_own.at[:, 0], load_sem.at[1]),
        pltpu.make_async_copy(v_hbm, kv_own.at[:, 1], load_sem.at[2]),
        pltpu.make_async_copy(q_hbm, q_ref, load_sem.at[3]),
    ]
    for load in loads:
        load.start()

    barrier = pltpu.get_barrier_semaphore()
    peers = (zu, zd, yu, yd, yf, z2, z6, z4, sibling, xu, xd)
    for peer in peers:
        pl.semaphore_signal(barrier, inc=1, device_id=peer, device_id_type=MESH)
    pl.semaphore_wait(barrier, len(peers))

    sent = []

    def send(src, dst, ssem, rsem, device, where=None):
        copy = pltpu.make_async_remote_copy(
            src_ref=src, dst_ref=dst, send_sem=ssem, recv_sem=rsem,
            device_id=device, device_id_type=MESH,
        )
        if where is None:
            copy.start()
        else:
            pl.when(where)(copy.start)
        sent.append((copy, where))

    def arrived(dst, rsem):
        pltpu.make_async_copy(dst, dst, rsem).wait()

    slots = [z, z_dn, z_up, (z + 6) % NZ, (z + 2) % NZ, (z + 5) % NZ, (z + 3) % NZ, (z + 4) % NZ]

    def spread(e):
        ref = w_own.at[y, slots[e]]
        send(ref, ref, yu_s.at[e], yu_r.at[e], yu)
        send(ref, ref, yd_s.at[e], yd_r.at[e], yd)

    def z_step(t):
        if t > 0:
            arrived(w_own.at[y, slots[2 * t - 1]], zu_r.at[t - 1])
        if t < 4:
            ref = w_own.at[y, z if t == 0 else slots[2 * t - 1]]
            send(ref, ref, zu_s.at[t], zu_r.at[t], zu)
        if 0 < t < 4:
            arrived(w_own.at[y, slots[2 * t]], zd_r.at[t - 1])
        if t < 3:
            ref = w_own.at[y, slots[2 * t]]
            send(ref, ref, zd_s.at[t], zd_r.at[t], zd)
        if t == 0:
            spread(0)
        else:
            spread(2 * t - 1)
            if t < 4:
                spread(2 * t)

    def y_step(e):
        low, high = w_own.at[y_dn, slots[e]], w_own.at[y_up, slots[e]]
        arrived(low, yu_r.at[e])
        if e % 2 == 0:
            send(low, low, far_s.at[e], far_r.at[e], yu)
        arrived(high, yd_r.at[e])
        if e % 2 == 1:
            send(high, high, far_s.at[e], far_r.at[e], yd)

    def far_step(e):
        arrived(w_own.at[y_far, slots[e]], far_r.at[e])
        send(w_own.at[:, slots[e]], w_sib.at[:, slots[e]], sib_s.at[e], sib_r.at[e], sibling)

    def chunk(s):
        return (x + ORDER[s]) % NX

    def kv_own_send(s):
        i = chunk(s)
        mine = kv_own.at[i]
        send(mine, kv_in.at[3, i], kv_s.at[1, s], kv_r.at[3, s], z2, inner)
        send(mine, kv_in.at[2, i], kv_s.at[0, s], kv_r.at[2, s], z1)
        send(mine, kv_in.at[0, i], kv_s.at[2, s], kv_r.at[0, s], y1)

    def kv_relay1(s):
        i = chunk(s)
        near = kv_in.at[2, i]
        arrived(near, kv_r.at[2, s])
        send(near, kv_in.at[3, i], kv_s.at[3, s], kv_r.at[3, s], z3, inner)
        near = kv_in.at[0, i]
        arrived(near, kv_r.at[0, s])
        send(near, kv_in.at[1, i], kv_s.at[5, s], kv_r.at[1, s], y3)

    def kv_relay2(s):
        i = chunk(s)
        mid = kv_in.at[3, i]
        arrived(mid, kv_r.at[3, s])
        send(mid, kv_in.at[4, i], kv_s.at[4, s], kv_r.at[4, s], z6)

    def kv_wait(s):
        i = chunk(s)
        for n in (1, 4):
            arrived(kv_in.at[n, i], kv_r.at[n, s])

    zpos = z // 4 + 2 * ((z // 2) % 2) + 4 * (z % 2)

    def pick():
        wanted = pos_ref[pl.ds(ctx // 4, 1), :]
        for part in range(2):
            picked = jnp.zeros((4 * PICK, HD), jnp.float32)
            for i in range(CHUNKS):
                spot = lax.broadcasted_iota(jnp.int32, (ROWS, 4 * PICK), 0) + (ctx * 1024 + i * ROWS)
                chosen = (spot == wanted).astype(jnp.float32).astype(jnp.bfloat16)
                picked += lax.dot_general(
                    chosen, kv_own[i, part], (((0,), (0,)), ((), ())),
                    preferred_element_type=jnp.float32,
                )
            pick_ref[...] = picked
            mine = pick_ref[pl.ds(pl.multiple_of((ctx % 4) * PICK, PICK), PICK), :]
            g_ref[part, y, pl.ds(pl.multiple_of(zpos * PICK, PICK), PICK), :] = mine.astype(jnp.bfloat16)

    def g_rows(yy, size, slot):
        start = (slot // size) * size * PICK
        return g_ref.at[:, yy, pl.ds(pl.multiple_of(start, size * PICK), size * PICK), :]

    def g_send(n):
        mine = g_rows(y, 1 << n, zpos)
        send(mine, mine, g_ssem.at[n], g_rsem.at[n], (z4, z2, z1)[n])

    def g_wait(n):
        arrived(g_rows(y, 1 << n, flip(zpos, 1 << n)), g_rsem.at[n])

    def g_y_send():
        whole = g_ref.at[:, y]
        for n, peer in enumerate((yu, yd, yf)):
            send(whole, whole, g_ssem.at[3 + n], g_rsem.at[3 + n], peer)

    def g_y_wait():
        for n, yy in enumerate((y_dn, y_up, y_far)):
            arrived(g_ref.at[:, yy], g_rsem.at[3 + n])

    def attend(i, t):
        j = 2 * i + t
        own = [j, flip(j, 1), flip(j, 2), flip(j, 4)]

        def block(part, n):
            if n < 4:
                jj = own[n]
                return kv_own[jj // 2, part, pl.ds(pl.multiple_of((jj % 2) * BLK, BLK), BLK), :]
            return kv_in[n - 4, i, part, pl.ds(t * BLK, BLK), :]

        rows = pl.ds(pl.multiple_of(j * BLK, BLK), BLK)
        queries = jnp.concatenate(
            [q_ref[rows, h * HD : (h + 1) * HD] for h in range(GROUPS)], axis=0
        )
        contract = (((1,), (1,)), ((), ()))

        def bias(n):
            return jnp.where(pairs_ref[j, n - 1] >= 0, 0.0, -jnp.inf).astype(jnp.float32)

        for first in range(0, 9, 2):
            names = list(range(first, min(first + 2, 9)))
            keys = jnp.concatenate([block(0, n) for n in names], axis=0)
            scores = lax.dot_general(queries, keys, contract, preferred_element_type=jnp.float32)
            for m, n in enumerate(names):
                part = scores[:, m * BLK : (m + 1) * BLK]
                if n > 0:
                    part = part + bias(n)
                s_ref[:, n * BLK : (n + 1) * BLK] = part
        for yy in range(NY):
            start = 9 * BLK + yy * NZ * PICK
            s_ref[:, start : start + NZ * PICK] = lax.dot_general(
                queries, g_ref[0, yy], contract, preferred_element_type=jnp.float32
            )
        totals = []
        for r in range(0, GROUPS * BLK, 64):
            scores = s_ref[r : r + 64, :]
            top = jnp.max(scores, axis=1, keepdims=True)
            weights = jnp.exp2((scores - top) * SCALE)
            totals.append(jnp.sum(weights, axis=1, keepdims=True))
            p_ref[r : r + 64, :] = weights.astype(jnp.bfloat16)
        values = jnp.concatenate(
            [block(1, n) for n in range(9)] + [g_ref[1, yy] for yy in range(NY)], axis=0
        )
        result = jnp.dot(p_ref[...], values, preferred_element_type=jnp.float32)
        result = (result / jnp.concatenate(totals, axis=0)).astype(jnp.bfloat16)
        for h in range(GROUPS):
            att_ref[i, t, :, h * HD : (h + 1) * HD] = result[h * BLK : (h + 1) * BLK]

    def pass_on(s):
        i = chunk(s)
        send(att_ref.at[i, 1 - core], att_in.at[i], att_s.at[s], att_r.at[s], sibling)

    def project(i, e, extra, put):
        left, right = att_ref[i, core], att_in[i]
        for half in range(2):
            zz, yy = slots[e], 2 * half
            columns = slice(half * 256, half * 256 + 256)
            total = jnp.dot(
                left, jnp.concatenate([w_own[yy, zz], w_own[yy + 1, zz]], axis=1),
                preferred_element_type=jnp.float32,
            ) + jnp.dot(
                right, jnp.concatenate([w_sib[yy, zz], w_sib[yy + 1, zz]], axis=1),
                preferred_element_type=jnp.float32,
            )
            if extra is not None:
                total = total + extra[:, columns].astype(jnp.float32)
            put(columns, total)

    def project_send(n, i, e, extra, dst, ssem, rsem, device):
        def put(columns, total):
            p_send[n, e, :, columns] = total.astype(jnp.bfloat16)

        project(i, e, extra, put)
        send(p_send.at[n, e], dst, ssem, rsem, device)

    def w_wait(e):
        arrived(w_sib.at[:, slots[e]], sib_r.at[e])

    def att_wait(s):
        arrived(att_in.at[chunk(s)], att_r.at[s])

    def p_far(e):
        dst, device = (r1a, xu) if e % 2 == 0 else (r1b, xd)
        project_send(0, chunk(0), e, None, dst.at[e // 2], one_s.at[e], one_r.at[e], device)

    def p_up(e):
        extra = None
        if e % 2 == 0:
            extra = r1a.at[e // 2]
            arrived(extra, one_r.at[e])
        project_send(1, chunk(1), e, extra, r2a.at[e], two_s.at[e], two_r.at[e], xu)

    def p_down(e):
        extra = None
        if e % 2 == 1:
            extra = r1b.at[e // 2]
            arrived(extra, one_r.at[e])
        project_send(2, chunk(2), e, extra, r2b.at[e], two_s.at[8 + e], two_r.at[8 + e], xd)

    def p_mine(e):
        def put(columns, total):
            acc_ref[e, :, columns] = total

        project(chunk(3), e, None, put)

    def finish(e):
        arrived(r2a.at[e], two_r.at[e])
        arrived(r2b.at[e], two_r.at[8 + e])
        columns = pl.ds(pl.multiple_of(slots[e] * 512, 512), 512)
        out_ref[:, columns] = (
            acc_ref[e] + r2a[e].astype(jnp.float32) + r2b[e].astype(jnp.float32)
        ).astype(jnp.bfloat16)

    def attend_step(s, t):
        attend(chunk(s), t)

    loads[0].wait()
    z_step(0)
    loads[1].wait()
    loads[2].wait()
    kv_own_send(0)
    pick()
    g_send(0)
    kv_relay1(0)
    g_wait(0)
    g_send(1)
    z_step(1)
    kv_own_send(1)
    kv_relay2(0)
    g_wait(1)
    g_send(2)
    z_step(2)
    g_wait(2)
    g_y_send()
    z_step(3)
    kv_relay1(1)
    z_step(4)
    y_step(0)
    y_step(1)
    kv_wait(0)
    g_y_wait()
    loads[3].wait()
    kv_own_send(2)
    attend_step(0, 0)
    kv_relay2(1)
    y_step(2)
    attend_step(0, 1)
    pass_on(0)
    y_step(3)
    kv_relay1(2)
    kv_wait(1)
    kv_own_send(3)
    attend_step(1, 0)
    kv_relay2(2)
    y_step(4)
    far_step(0)
    far_step(1)
    attend_step(1, 1)
    pass_on(1)
    kv_relay1(3)
    y_step(5)
    att_wait(0)
    far_step(2)
    for e in range(2):
        w_wait(e)
        p_far(e)
    y_step(6)
    y_step(7)
    far_step(3)
    kv_relay2(3)
    kv_wait(2)
    attend_step(2, 0)
    far_step(4)
    for e in range(2, 4):
        w_wait(e)
        p_far(e)
    attend_step(2, 1)
    pass_on(2)
    far_step(5)
    far_step(6)
    far_step(7)
    for e in range(4, 8):
        w_wait(e)
        p_far(e)
    att_wait(1)
    att_wait(2)
    for e in range(4):
        p_up(2 * e + 1)
        p_down(2 * e)
    for e in range(2):
        p_up(2 * e)
        p_down(2 * e + 1)
    kv_wait(3)
    attend_step(3, 0)
    for e in range(2, 4):
        p_up(2 * e)
        p_down(2 * e + 1)
    attend_step(3, 1)
    pass_on(3)
    att_wait(3)
    for e in range(8):
        p_mine(e)
    for e in (1, 0, 3, 2, 5, 4, 7, 6):
        finish(e)
    for copy, where in sent:
        if where is None:
            copy.wait_send()
        else:
            pl.when(where)(copy.wait_send)


def shards(queries, keys, values, pairs, positions, w_out):
    bf16, f32 = jnp.bfloat16, jnp.float32
    dma = pltpu.SemaphoreType.DMA
    hbm = pl.BlockSpec(memory_space=pl.ANY)
    return pl.pallas_call(
        kernel,
        out_shape=jax.ShapeDtypeStruct((BLK, 4096), bf16),
        in_specs=[
            hbm, hbm, hbm,
            pl.BlockSpec(memory_space=pltpu.SMEM),
            pl.BlockSpec(memory_space=pltpu.VMEM),
            hbm,
        ],
        out_specs=pl.BlockSpec(memory_space=pltpu.VMEM),
        scratch_shapes=[
            pltpu.VMEM((1024, GROUPS * HD), bf16),
            pltpu.VMEM((CHUNKS, 2, ROWS, HD), bf16),
            pltpu.VMEM((5, CHUNKS, 2, ROWS, HD), bf16),
            pltpu.VMEM((2, NY, NZ * PICK, HD), bf16),
            pltpu.VMEM((NY, NZ, 512, HD), bf16),
            pltpu.VMEM((NY, NZ, 512, HD), bf16),
            pltpu.VMEM((GROUPS * BLK, KEYS), f32),
            pltpu.VMEM((GROUPS * BLK, KEYS), bf16),
            pltpu.VMEM((CHUNKS, 2, BLK, GROUPS * HD), bf16),
            pltpu.VMEM((CHUNKS, BLK, GROUPS * HD), bf16),
            pltpu.VMEM((3, 8, BLK, 512), bf16),
            pltpu.VMEM((4, BLK, 512), bf16),
            pltpu.VMEM((4, BLK, 512), bf16),
            pltpu.VMEM((8, BLK, 512), bf16),
            pltpu.VMEM((8, BLK, 512), bf16),
            pltpu.VMEM((8, BLK, 512), f32),
            pltpu.VMEM((4 * PICK, HD), f32),
            dma((4,)), dma((6, CHUNKS)), dma((5, CHUNKS)), dma((6,)), dma((6,)),
            dma((4,)), dma((4,)), dma((3,)), dma((3,)),
            dma((8,)), dma((8,)), dma((8,)), dma((8,)), dma((8,)), dma((8,)),
            dma((8,)), dma((8,)), dma((4,)), dma((4,)),
            dma((8,)), dma((8,)), dma((16,)), dma((16,)),
        ],
        compiler_params=pltpu.CompilerParams(
            collective_id=0, has_side_effects=True, vmem_limit_bytes=56 * 2**20
        ),
        name="butterfly",
    )(
        queries,
        keys.reshape(CHUNKS, ROWS, HD),
        values.reshape(CHUNKS, ROWS, HD),
        pairs,
        positions.reshape(BLOCKS, NY * NZ * PICK // BLOCKS),
        w_out,
    )


def solution(mesh):
    return jax.shard_map(
        shards,
        mesh=mesh,
        in_specs=(
            P("ctx", "head"),
            P("ctx", "head"),
            P("ctx", "head"),
            P("ctx", None),
            P(),
            P("head", "ctx"),
        ),
        out_specs=P(("ctx", "head"), None),
        check_vma=False,
    )
```

```python
import math

import jax
import jax.numpy as jnp
from jax import lax
from jax.experimental import pallas as pl
from jax.experimental.pallas import tpu as pltpu
from jax.sharding import PartitionSpec as P

HD = 128
BLK = 128
BLOCKS = 8
CHUNKS = 4
ROWS = 2 * BLK
GROUPS = 4
NY, NZ, NX = 4, 8, 4
PICK = 32
KEYS = 9 * BLK + NY * NZ * PICK
SCALE = math.log2(math.e) / math.sqrt(HD)
MESH = pl.DeviceIdType.MESH
ORDER = (2, 1, 3, 0)


def flip(value, span):
    return value + span - 2 * span * ((value // span) % 2)


def kernel(
    q_hbm, k_hbm, v_hbm, pairs_ref, pos_ref, w_hbm, out_ref,
    q_ref, kv_own, kv_in, g_ref, w_own, w_sib, s_ref, p_ref, att_ref, att_in,
    p_send, r1a, r1b, r2a, r2b, acc_ref, pick_ref,
    load_sem, kv_s, kv_r, g_ssem, g_rsem, zu_s, zu_r, zd_s, zd_r,
    yu_s, yu_r, yd_s, yd_r, far_s, far_r, sib_s, sib_r, att_s, att_r,
    one_s, one_r, two_s, two_r,
):
    ctx = lax.axis_index("ctx")
    head = lax.axis_index("head")
    z, y = ctx // NY, ctx % NY
    x, core = head // 2, head % 2

    def at(zz, yy):
        return (zz * NY + yy, head)

    z_up, z_dn = (z + 1) % NZ, (z + NZ - 1) % NZ
    y_up, y_dn, y_far = (y + 1) % NY, (y + NY - 1) % NY, (y + 2) % NY
    zu, zd, yu, yd, yf = at(z_up, y), at(z_dn, y), at(z, y_up), at(z, y_dn), at(z, y_far)
    sibling = (ctx, flip(head, 1))
    xu = (ctx, ((x + 1) % NX) * 2 + core)
    xd = (ctx, ((x + NX - 1) % NX) * 2 + core)
    z_far = (z + 4) % NZ
    z1, z2 = at(flip(z, 1), y), at(flip(z, 2), y)
    z3, z6 = at(flip(flip(z, 1), 2), y), at(flip(z_far, 2), y)
    along = [(k, (z + k) % NZ) for k in (1, 7, 2, 6, 3, 5, 4)]
    zu2, zd2 = at((z + 2) % NZ, y), at((z + 6) % NZ, y)
    y1, y3 = at(z, flip(y, 1)), at(z, flip((y + 2) % NY, 1))
    inner = ((z + 1) // 2) % 2 == 1

    loads = [
        pltpu.make_async_copy(w_hbm, w_own.at[y, z], load_sem.at[0]),
        pltpu.make_async_copy(k_hbm, kv_own.at[:, 0], load_sem.at[1]),
        pltpu.make_async_copy(v_hbm, kv_own.at[:, 1], load_sem.at[2]),
        pltpu.make_async_copy(q_hbm, q_ref, load_sem.at[3]),
    ]
    for load in loads:
        load.start()

    barrier = pltpu.get_barrier_semaphore()
    peers = [at(zz, y) for _, zz in along] + [yu, yd, yf, sibling, xu, xd]
    for peer in peers:
        pl.semaphore_signal(barrier, inc=1, device_id=peer, device_id_type=MESH)
    pl.semaphore_wait(barrier, len(peers))

    sent = []

    def send(src, dst, ssem, rsem, device, where=None):
        copy = pltpu.make_async_remote_copy(
            src_ref=src, dst_ref=dst, send_sem=ssem, recv_sem=rsem,
            device_id=device, device_id_type=MESH,
        )
        if where is None:
            copy.start()
        else:
            pl.when(where)(copy.start)
        sent.append((copy, where))

    def arrived(dst, rsem):
        pltpu.make_async_copy(dst, dst, rsem).wait()

    slots = [z, z_dn, z_up, (z + 6) % NZ, (z + 2) % NZ, (z + 5) % NZ, (z + 3) % NZ, (z + 4) % NZ]

    def spread(e):
        ref = w_own.at[y, slots[e]]
        send(ref, ref, yu_s.at[e], yu_r.at[e], yu)
        send(ref, ref, yd_s.at[e], yd_r.at[e], yd)

    def z_forth(t):
        ref = w_own.at[y, z if t == 0 else slots[2 * t - 1]]
        if t > 0:
            arrived(ref, zu_r.at[t - 1])
        if t < 4:
            send(ref, ref, zu_s.at[t], zu_r.at[t], zu)

    def z_back(t):
        ref = w_own.at[y, slots[2 * t]]
        if t > 0:
            arrived(ref, zd_r.at[t - 1])
        if t < 3:
            send(ref, ref, zd_s.at[t], zd_r.at[t], zd)

    def y_low(e):
        low = w_own.at[y_dn, slots[e]]
        arrived(low, yu_r.at[e])
        if e % 2 == 0:
            send(low, low, far_s.at[e], far_r.at[e], yu)

    def y_high(e):
        high = w_own.at[y_up, slots[e]]
        arrived(high, yd_r.at[e])
        if e % 2 == 1:
            send(high, high, far_s.at[e], far_r.at[e], yd)

    def far_step(e):
        arrived(w_own.at[y_far, slots[e]], far_r.at[e])
        send(w_own.at[:, slots[e]], w_sib.at[:, slots[e]], sib_s.at[e], sib_r.at[e], sibling)

    def chunk(s):
        return (x + ORDER[s]) % NX

    def kv_own_z(s):
        i = chunk(s)
        mine = kv_own.at[i]
        send(mine, kv_in.at[3, i], kv_s.at[1, s], kv_r.at[3, s], z2, inner)
        send(mine, kv_in.at[2, i], kv_s.at[0, s], kv_r.at[2, s], z1)

    def kv_own_y(s):
        i = chunk(s)
        send(kv_own.at[i], kv_in.at[0, i], kv_s.at[2, s], kv_r.at[0, s], y1)

    def kv_relay_z(s):
        i = chunk(s)
        near = kv_in.at[2, i]
        arrived(near, kv_r.at[2, s])
        send(near, kv_in.at[3, i], kv_s.at[3, s], kv_r.at[3, s], z3, inner)

    def kv_relay_y(s):
        i = chunk(s)
        near = kv_in.at[0, i]
        arrived(near, kv_r.at[0, s])
        send(near, kv_in.at[1, i], kv_s.at[5, s], kv_r.at[1, s], y3)

    def kv_relay2(s):
        i = chunk(s)
        mid = kv_in.at[3, i]
        arrived(mid, kv_r.at[3, s])
        send(mid, kv_in.at[4, i], kv_s.at[4, s], kv_r.at[4, s], z6)

    def kv_wait_y(s):
        arrived(kv_in.at[1, chunk(s)], kv_r.at[1, s])

    def kv_wait_z(s):
        arrived(kv_in.at[4, chunk(s)], kv_r.at[4, s])

    def pick():
        wanted = pos_ref[pl.ds(ctx // 4, 1), :]
        for part in range(2):
            picked = jnp.zeros((4 * PICK, HD), jnp.float32)
            for i in range(CHUNKS):
                spot = lax.broadcasted_iota(jnp.int32, (ROWS, 4 * PICK), 0) + (ctx * 1024 + i * ROWS)
                chosen = (spot == wanted).astype(jnp.float32).astype(jnp.bfloat16)
                picked += lax.dot_general(
                    chosen, kv_own[i, part], (((0,), (0,)), ((), ())),
                    preferred_element_type=jnp.float32,
                )
            pick_ref[...] = picked
            mine = pick_ref[pl.ds(pl.multiple_of((ctx % 4) * PICK, PICK), PICK), :]
            g_ref[part, y, pl.ds(pl.multiple_of(z * PICK, PICK), PICK), :] = mine.astype(jnp.bfloat16)

    def g_rows(zz):
        return g_ref.at[:, y, pl.ds(pl.multiple_of(zz * PICK, PICK), PICK), :]

    def g_send():
        for k, zz in along:
            send(g_rows(z), g_rows(z), g_ssem.at[2 + k], g_rsem.at[2 + k], at(zz, y))

    def g_wait():
        for k, _ in along:
            arrived(g_rows((z + NZ - k) % NZ), g_rsem.at[2 + k])

    def g_y_send():
        whole = g_ref.at[:, y]
        for n, peer in enumerate((yu, yd, yf)):
            send(whole, whole, g_ssem.at[n], g_rsem.at[n], peer)

    def g_y_wait():
        for n, yy in enumerate((y_dn, y_up, y_far)):
            arrived(g_ref.at[:, yy], g_rsem.at[n])

    def attend(i, t):
        j = 2 * i + t
        own = [j, flip(j, 1), flip(j, 2), flip(j, 4)]

        def block(part, n):
            if n < 4:
                jj = own[n]
                return kv_own[jj // 2, part, pl.ds(pl.multiple_of((jj % 2) * BLK, BLK), BLK), :]
            return kv_in[n - 4, i, part, pl.ds(pl.multiple_of(t * BLK, BLK), BLK), :]

        rows = pl.ds(pl.multiple_of(j * BLK, BLK), BLK)
        queries = jnp.concatenate(
            [q_ref[rows, h * HD : (h + 1) * HD] for h in range(GROUPS)], axis=0
        )
        contract = (((1,), (1,)), ((), ()))

        def bias(n):
            return jnp.where(pairs_ref[j, n - 1] >= 0, 0.0, -jnp.inf).astype(jnp.float32)

        for first in range(0, 9, 2):
            names = list(range(first, min(first + 2, 9)))
            keys = jnp.concatenate([block(0, n) for n in names], axis=0)
            scores = lax.dot_general(queries, keys, contract, preferred_element_type=jnp.float32)
            for m, n in enumerate(names):
                part = scores[:, m * BLK : (m + 1) * BLK]
                if n > 0:
                    part = part + bias(n)
                s_ref[:, n * BLK : (n + 1) * BLK] = part
        for yy in range(NY):
            start = 9 * BLK + yy * NZ * PICK
            s_ref[:, start : start + NZ * PICK] = lax.dot_general(
                queries, g_ref[0, yy], contract, preferred_element_type=jnp.float32
            )
        totals = []
        for r in range(0, GROUPS * BLK, 64):
            scores = s_ref[r : r + 64, :]
            top = jnp.max(scores, axis=1, keepdims=True)
            weights = jnp.exp2((scores - top) * SCALE)
            totals.append(jnp.sum(weights, axis=1, keepdims=True))
            p_ref[r : r + 64, :] = weights.astype(jnp.bfloat16)
        values = jnp.concatenate(
            [block(1, n) for n in range(9)] + [g_ref[1, yy] for yy in range(NY)], axis=0
        )
        result = jnp.dot(p_ref[...], values, preferred_element_type=jnp.float32)
        result = (result / jnp.concatenate(totals, axis=0)).astype(jnp.bfloat16)
        for h in range(GROUPS):
            att_ref[i, t, :, h * HD : (h + 1) * HD] = result[h * BLK : (h + 1) * BLK]

    def pass_on(s):
        i = chunk(s)
        send(att_ref.at[i, 1 - core], att_in.at[i], att_s.at[s], att_r.at[s], sibling)

    def project(i, e, extra, put):
        left, right = att_ref[i, core], att_in[i]
        for half in range(2):
            zz, yy = slots[e], 2 * half
            columns = slice(half * 256, half * 256 + 256)
            total = jnp.dot(
                left, jnp.concatenate([w_own[yy, zz], w_own[yy + 1, zz]], axis=1),
                preferred_element_type=jnp.float32,
            ) + jnp.dot(
                right, jnp.concatenate([w_sib[yy, zz], w_sib[yy + 1, zz]], axis=1),
                preferred_element_type=jnp.float32,
            )
            if extra is not None:
                total = total + extra[:, columns].astype(jnp.float32)
            put(columns, total)

    def project_send(n, i, e, extra, dst, ssem, rsem, device):
        def put(columns, total):
            p_send[n, e, :, columns] = total.astype(jnp.bfloat16)

        project(i, e, extra, put)
        send(p_send.at[n, e], dst, ssem, rsem, device)

    def w_wait(e):
        arrived(w_sib.at[:, slots[e]], sib_r.at[e])

    def att_wait(s):
        arrived(att_in.at[chunk(s)], att_r.at[s])

    def p_far(e):
        dst, device = (r1a, xu) if e % 2 == 0 else (r1b, xd)
        project_send(0, chunk(0), e, None, dst.at[e // 2], one_s.at[e], one_r.at[e], device)

    def p_up(e):
        extra = None
        if e % 2 == 0:
            extra = r1a.at[e // 2]
            arrived(extra, one_r.at[e])
        project_send(1, chunk(1), e, extra, r2a.at[e], two_s.at[e], two_r.at[e], xu)

    def p_down(e):
        extra = None
        if e % 2 == 1:
            extra = r1b.at[e // 2]
            arrived(extra, one_r.at[e])
        project_send(2, chunk(2), e, extra, r2b.at[e], two_s.at[8 + e], two_r.at[8 + e], xd)

    def p_mine(e):
        def put(columns, total):
            acc_ref[e, :, columns] = total

        project(chunk(3), e, None, put)

    def finish(e):
        arrived(r2a.at[e], two_r.at[e])
        arrived(r2b.at[e], two_r.at[8 + e])
        columns = pl.ds(pl.multiple_of(slots[e] * 512, 512), 512)
        out_ref[:, columns] = (
            acc_ref[e] + r2a[e].astype(jnp.float32) + r2b[e].astype(jnp.float32)
        ).astype(jnp.bfloat16)

    def attend_first(s):
        attend(chunk(s), 1 - core)
        pass_on(s)

    def attend_last(s):
        attend(chunk(s), core)

    loads[1].wait()
    loads[2].wait()
    kv_own_y(1)
    loads[0].wait()
    z_forth(0)
    z_back(0)
    spread(0)
    pick()
    g_send()
    z_forth(1)
    z_back(1)
    kv_own_y(0)
    spread(1)
    spread(2)
    z_forth(2)
    y_high(0)
    kv_own_z(0)
    spread(3)
    z_back(2)
    g_wait()
    y_high(1)
    g_y_send()
    kv_relay_y(1)
    z_forth(3)
    y_low(3)
    z_forth(4)
    kv_relay_y(0)
    y_high(3)
    kv_relay_z(0)
    kv_own_z(1)
    y_high(2)
    y_low(0)
    kv_own_y(2)
    kv_own_z(2)
    kv_relay2(0)
    spread(4)
    spread(5)
    kv_relay_z(1)
    z_back(3)
    kv_relay_z(2)
    kv_wait_y(0)
    y_low(2)
    far_step(3)
    y_low(1)
    kv_relay_y(2)
    kv_relay2(1)
    far_step(0)
    spread(7)
    y_high(5)
    spread(6)
    w_wait(3)
    far_step(1)
    kv_wait_z(0)
    g_y_wait()
    y_low(4)
    kv_wait_y(1)
    loads[3].wait()
    attend_first(0)
    kv_own_y(3)
    attend_last(0)
    att_wait(0)
    kv_wait_z(1)
    w_wait(1)
    kv_relay2(2)
    y_low(5)
    far_step(2)
    w_wait(0)
    attend_first(1)
    p_far(0)
    p_far(3)
    far_step(5)
    p_far(1)
    w_wait(2)
    p_far(2)
    kv_own_z(3)
    attend_last(1)
    y_high(7)
    y_low(6)
    kv_wait_y(2)
    w_wait(5)
    y_high(6)
    kv_wait_z(2)
    y_high(4)
    att_wait(1)
    p_up(5)
    p_far(5)
    attend_first(2)
    kv_relay_z(3)
    far_step(4)
    y_low(7)
    attend_last(2)
    p_up(3)
    att_wait(2)
    far_step(6)
    p_down(2)
    p_down(3)
    kv_relay_y(3)
    kv_relay2(3)
    far_step(7)
    p_up(0)
    w_wait(6)
    w_wait(4)
    w_wait(7)
    p_far(4)
    p_far(7)
    p_far(6)
    kv_wait_y(3)
    p_down(0)
    p_up(1)
    p_down(1)
    kv_wait_z(3)
    attend_first(3)
    attend_last(3)
    p_up(2)
    att_wait(3)
    p_up(6)
    p_up(7)
    p_down(5)
    p_mine(3)
    p_up(4)
    p_mine(0)
    p_down(7)
    p_mine(1)
    finish(3)
    p_mine(4)
    p_mine(6)
    p_down(6)
    p_mine(2)
    p_down(4)
    finish(2)
    p_mine(7)
    finish(7)
    finish(0)
    p_mine(5)
    finish(1)
    finish(6)
    finish(5)
    finish(4)
    for copy, where in sent:
        if where is None:
            copy.wait_send()
        else:
            pl.when(where)(copy.wait_send)


def shards(queries, keys, values, pairs, positions, w_out):
    bf16, f32 = jnp.bfloat16, jnp.float32
    dma = pltpu.SemaphoreType.DMA
    hbm = pl.BlockSpec(memory_space=pl.ANY)
    return pl.pallas_call(
        kernel,
        out_shape=jax.ShapeDtypeStruct((BLK, 4096), bf16),
        in_specs=[
            hbm, hbm, hbm,
            pl.BlockSpec(memory_space=pltpu.SMEM),
            pl.BlockSpec(memory_space=pltpu.VMEM),
            hbm,
        ],
        out_specs=pl.BlockSpec(memory_space=pltpu.VMEM),
        scratch_shapes=[
            pltpu.VMEM((1024, GROUPS * HD), bf16),
            pltpu.VMEM((CHUNKS, 2, ROWS, HD), bf16),
            pltpu.VMEM((5, CHUNKS, 2, ROWS, HD), bf16),
            pltpu.VMEM((2, NY, NZ * PICK, HD), bf16),
            pltpu.VMEM((NY, NZ, 512, HD), bf16),
            pltpu.VMEM((NY, NZ, 512, HD), bf16),
            pltpu.VMEM((GROUPS * BLK, KEYS), f32),
            pltpu.VMEM((GROUPS * BLK, KEYS), bf16),
            pltpu.VMEM((CHUNKS, 2, BLK, GROUPS * HD), bf16),
            pltpu.VMEM((CHUNKS, BLK, GROUPS * HD), bf16),
            pltpu.VMEM((3, 8, BLK, 512), bf16),
            pltpu.VMEM((4, BLK, 512), bf16),
            pltpu.VMEM((4, BLK, 512), bf16),
            pltpu.VMEM((8, BLK, 512), bf16),
            pltpu.VMEM((8, BLK, 512), bf16),
            pltpu.VMEM((8, BLK, 512), f32),
            pltpu.VMEM((4 * PICK, HD), f32),
            dma((4,)), dma((6, CHUNKS)), dma((5, CHUNKS)), dma((10,)), dma((10,)),
            dma((4,)), dma((4,)), dma((4,)), dma((4,)),
            dma((8,)), dma((8,)), dma((8,)), dma((8,)), dma((8,)), dma((8,)),
            dma((8,)), dma((8,)), dma((4,)), dma((4,)),
            dma((8,)), dma((8,)), dma((16,)), dma((16,)),
        ],
        compiler_params=pltpu.CompilerParams(
            collective_id=0, has_side_effects=True, vmem_limit_bytes=56 * 2**20
        ),
        name="butterfly",
    )(
        queries,
        keys.reshape(CHUNKS, ROWS, HD),
        values.reshape(CHUNKS, ROWS, HD),
        pairs,
        positions.reshape(BLOCKS, NY * NZ * PICK // BLOCKS),
        w_out,
    )


def solution(mesh):
    return jax.shard_map(
        shards,
        mesh=mesh,
        in_specs=(
            P("ctx", "head"),
            P("ctx", "head"),
            P("ctx", "head"),
            P("ctx", None),
            P(),
            P("head", "ctx"),
        ),
        out_specs=P(("ctx", "head"), None),
        check_vma=False,
    )
```

```python
import math

import jax
import jax.numpy as jnp
from jax import lax
from jax.experimental import pallas as pl
from jax.experimental.pallas import tpu as pltpu
from jax.sharding import PartitionSpec as P

HD = 128
BLK = 128
BLOCKS = 8
CHUNKS = 4
ROWS = 2 * BLK
GROUPS = 4
NY, NZ, NX = 4, 8, 4
PICK = 32
KEYS = 9 * BLK + NY * NZ * PICK
SCALE = math.log2(math.e) / math.sqrt(HD)
MESH = pl.DeviceIdType.MESH
ORDER = (2, 1, 3, 0)


def flip(value, span):
    return value + span - 2 * span * ((value // span) % 2)


def kernel(
    q_hbm, k_hbm, v_hbm, pairs_ref, pos_ref, w_hbm, out_ref,
    q_ref, kv_own, kv_in, g_ref, w_own, w_sib, s_ref, p_ref, att_ref, att_in,
    p_send, r1a, r1b, r2a, r2b, acc_ref, pick_ref,
    load_sem, kv_s, kv_r, g_ssem, g_rsem, zu_s, zu_r, zd_s, zd_r,
    yu_s, yu_r, yd_s, yd_r, far_s, far_r, sib_s, sib_r, att_s, att_r,
    one_s, one_r, two_s, two_r,
):
    ctx = lax.axis_index("ctx")
    head = lax.axis_index("head")
    z, y = ctx // NY, ctx % NY
    x, core = head // 2, head % 2

    def at(zz, yy):
        return (zz * NY + yy, head)

    z_up, z_dn = (z + 1) % NZ, (z + NZ - 1) % NZ
    y_up, y_dn, y_far = (y + 1) % NY, (y + NY - 1) % NY, (y + 2) % NY
    zu, zd, yu, yd, yf = at(z_up, y), at(z_dn, y), at(z, y_up), at(z, y_dn), at(z, y_far)
    sibling = (ctx, flip(head, 1))
    xu = (ctx, ((x + 1) % NX) * 2 + core)
    xd = (ctx, ((x + NX - 1) % NX) * 2 + core)
    z_far = (z + 4) % NZ
    z1, z2 = at(flip(z, 1), y), at(flip(z, 2), y)
    z3, z6 = at(flip(flip(z, 1), 2), y), at(flip(z_far, 2), y)
    along = [(k, (z + k) % NZ) for k in (1, 7, 2, 6, 3, 5, 4)]
    zu2, zd2 = at((z + 2) % NZ, y), at((z + 6) % NZ, y)
    y1, y3 = at(z, flip(y, 1)), at(z, flip((y + 2) % NY, 1))
    inner = ((z + 1) // 2) % 2 == 1

    loads = [
        pltpu.make_async_copy(w_hbm, w_own.at[y, z], load_sem.at[0]),
        pltpu.make_async_copy(k_hbm, kv_own.at[:, 0], load_sem.at[1]),
        pltpu.make_async_copy(v_hbm, kv_own.at[:, 1], load_sem.at[2]),
        pltpu.make_async_copy(q_hbm, q_ref, load_sem.at[3]),
    ]
    for load in loads:
        load.start()

    barrier = pltpu.get_barrier_semaphore()
    peers = [at(zz, y) for _, zz in along] + [yu, yd, yf, sibling, xu, xd]
    for peer in peers:
        pl.semaphore_signal(barrier, inc=1, device_id=peer, device_id_type=MESH)
    pl.semaphore_wait(barrier, len(peers))

    sent = []

    def send(src, dst, ssem, rsem, device, where=None):
        copy = pltpu.make_async_remote_copy(
            src_ref=src, dst_ref=dst, send_sem=ssem, recv_sem=rsem,
            device_id=device, device_id_type=MESH,
        )
        if where is None:
            copy.start()
        else:
            pl.when(where)(copy.start)
        sent.append((copy, where))

    def settle(keep):
        done = len(sent) - keep
        for copy, where in sent[:done]:
            if where is None:
                copy.wait_send()
            else:
                pl.when(where)(copy.wait_send)
        del sent[:done]

    def arrived(dst, rsem):
        pltpu.make_async_copy(dst, dst, rsem).wait()

    slots = [z, z_dn, z_up, (z + 6) % NZ, (z + 2) % NZ, (z + 5) % NZ, (z + 3) % NZ, (z + 4) % NZ]

    def spread(e):
        ref = w_own.at[y, slots[e]]
        send(ref, ref, yu_s.at[e], yu_r.at[e], yu)
        send(ref, ref, yd_s.at[e], yd_r.at[e], yd)

    def z_forth(t):
        ref = w_own.at[y, z if t == 0 else slots[2 * t - 1]]
        if t > 0:
            arrived(ref, zu_r.at[t - 1])
        if t < 4:
            send(ref, ref, zu_s.at[t], zu_r.at[t], zu)

    def z_back(t):
        ref = w_own.at[y, slots[2 * t]]
        if t > 0:
            arrived(ref, zd_r.at[t - 1])
        if t < 3:
            send(ref, ref, zd_s.at[t], zd_r.at[t], zd)

    def y_low(e):
        low = w_own.at[y_dn, slots[e]]
        arrived(low, yu_r.at[e])
        if e % 2 == 0:
            send(low, low, far_s.at[e], far_r.at[e], yu)

    def y_high(e):
        high = w_own.at[y_up, slots[e]]
        arrived(high, yd_r.at[e])
        if e % 2 == 1:
            send(high, high, far_s.at[e], far_r.at[e], yd)

    def far_step(e):
        arrived(w_own.at[y_far, slots[e]], far_r.at[e])
        send(w_own.at[:, slots[e]], w_sib.at[:, slots[e]], sib_s.at[e], sib_r.at[e], sibling)

    def chunk(s):
        return (x + ORDER[s]) % NX

    def kv_own_z(s):
        i = chunk(s)
        mine = kv_own.at[i]
        send(mine, kv_in.at[3, i], kv_s.at[1, s], kv_r.at[3, s], z2, inner)
        send(mine, kv_in.at[2, i], kv_s.at[0, s], kv_r.at[2, s], z1)

    def kv_own_y(s):
        i = chunk(s)
        send(kv_own.at[i], kv_in.at[0, i], kv_s.at[2, s], kv_r.at[0, s], y1)

    def kv_relay_z(s):
        i = chunk(s)
        near = kv_in.at[2, i]
        arrived(near, kv_r.at[2, s])
        send(near, kv_in.at[3, i], kv_s.at[3, s], kv_r.at[3, s], z3, inner)

    def kv_relay_y(s):
        i = chunk(s)
        near = kv_in.at[0, i]
        arrived(near, kv_r.at[0, s])
        send(near, kv_in.at[1, i], kv_s.at[5, s], kv_r.at[1, s], y3)

    def kv_relay2(s):
        i = chunk(s)
        mid = kv_in.at[3, i]
        arrived(mid, kv_r.at[3, s])
        send(mid, kv_in.at[4, i], kv_s.at[4, s], kv_r.at[4, s], z6)

    def kv_wait_y(s):
        arrived(kv_in.at[1, chunk(s)], kv_r.at[1, s])

    def kv_wait_z(s):
        arrived(kv_in.at[4, chunk(s)], kv_r.at[4, s])

    def pick():
        wanted = pos_ref[pl.ds(ctx // 4, 1), :]
        for part in range(2):
            picked = jnp.zeros((4 * PICK, HD), jnp.float32)
            for i in range(CHUNKS):
                spot = lax.broadcasted_iota(jnp.int32, (ROWS, 4 * PICK), 0) + (ctx * 1024 + i * ROWS)
                chosen = (spot == wanted).astype(jnp.float32).astype(jnp.bfloat16)
                picked += lax.dot_general(
                    chosen, kv_own[i, part], (((0,), (0,)), ((), ())),
                    preferred_element_type=jnp.float32,
                )
            pick_ref[...] = picked
            mine = pick_ref[pl.ds(pl.multiple_of((ctx % 4) * PICK, PICK), PICK), :]
            g_ref[part, y, pl.ds(pl.multiple_of(z * PICK, PICK), PICK), :] = mine.astype(jnp.bfloat16)

    def g_rows(zz):
        return g_ref.at[:, y, pl.ds(pl.multiple_of(zz * PICK, PICK), PICK), :]

    def g_send():
        for k, zz in along:
            send(g_rows(z), g_rows(z), g_ssem.at[2 + k], g_rsem.at[2 + k], at(zz, y))

    def g_wait():
        for k, _ in along:
            arrived(g_rows((z + NZ - k) % NZ), g_rsem.at[2 + k])

    def g_y_send():
        whole = g_ref.at[:, y]
        for n, peer in enumerate((yu, yd, yf)):
            send(whole, whole, g_ssem.at[n], g_rsem.at[n], peer)

    def g_y_wait():
        for n, yy in enumerate((y_dn, y_up, y_far)):
            arrived(g_ref.at[:, yy], g_rsem.at[n])

    def attend(i, t):
        j = 2 * i + t
        own = [j, flip(j, 1), flip(j, 2), flip(j, 4)]

        def block(part, n):
            if n < 4:
                jj = own[n]
                return kv_own[jj // 2, part, pl.ds(pl.multiple_of((jj % 2) * BLK, BLK), BLK), :]
            return kv_in[n - 4, i, part, pl.ds(pl.multiple_of(t * BLK, BLK), BLK), :]

        rows = pl.ds(pl.multiple_of(j * BLK, BLK), BLK)
        queries = jnp.concatenate(
            [q_ref[rows, h * HD : (h + 1) * HD] for h in range(GROUPS)], axis=0
        )
        contract = (((1,), (1,)), ((), ()))

        def bias(n):
            return jnp.where(pairs_ref[j, n - 1] >= 0, 0.0, -jnp.inf).astype(jnp.float32)

        for first in range(0, 9, 2):
            names = list(range(first, min(first + 2, 9)))
            keys = jnp.concatenate([block(0, n) for n in names], axis=0)
            scores = lax.dot_general(queries, keys, contract, preferred_element_type=jnp.float32)
            for m, n in enumerate(names):
                part = scores[:, m * BLK : (m + 1) * BLK]
                if n > 0:
                    part = part + bias(n)
                s_ref[:, n * BLK : (n + 1) * BLK] = part
        for yy in range(NY):
            start = 9 * BLK + yy * NZ * PICK
            s_ref[:, start : start + NZ * PICK] = lax.dot_general(
                queries, g_ref[0, yy], contract, preferred_element_type=jnp.float32
            )
        totals = []
        for r in range(0, GROUPS * BLK, 64):
            scores = s_ref[r : r + 64, :]
            top = jnp.max(scores, axis=1, keepdims=True)
            weights = jnp.exp2((scores - top) * SCALE)
            totals.append(jnp.sum(weights, axis=1, keepdims=True))
            p_ref[r : r + 64, :] = weights.astype(jnp.bfloat16)
        values = jnp.concatenate(
            [block(1, n) for n in range(9)] + [g_ref[1, yy] for yy in range(NY)], axis=0
        )
        result = jnp.dot(p_ref[...], values, preferred_element_type=jnp.float32)
        result = (result / jnp.concatenate(totals, axis=0)).astype(jnp.bfloat16)
        for h in range(GROUPS):
            att_ref[i, t, :, h * HD : (h + 1) * HD] = result[h * BLK : (h + 1) * BLK]

    def pass_on(s):
        i = chunk(s)
        send(att_ref.at[i, 1 - core], att_in.at[i], att_s.at[s], att_r.at[s], sibling)

    def project(i, e, extra, put):
        left, right = att_ref[i, core], att_in[i]
        for half in range(2):
            zz, yy = slots[e], 2 * half
            columns = slice(half * 256, half * 256 + 256)
            total = jnp.dot(
                left, jnp.concatenate([w_own[yy, zz], w_own[yy + 1, zz]], axis=1),
                preferred_element_type=jnp.float32,
            ) + jnp.dot(
                right, jnp.concatenate([w_sib[yy, zz], w_sib[yy + 1, zz]], axis=1),
                preferred_element_type=jnp.float32,
            )
            if extra is not None:
                total = total + extra[:, columns].astype(jnp.float32)
            put(columns, total)

    def project_send(n, i, e, extra, dst, ssem, rsem, device):
        def put(columns, total):
            p_send[n, e, :, columns] = total.astype(jnp.bfloat16)

        project(i, e, extra, put)
        send(p_send.at[n, e], dst, ssem, rsem, device)

    def w_wait(e):
        arrived(w_sib.at[:, slots[e]], sib_r.at[e])

    def att_wait(s):
        arrived(att_in.at[chunk(s)], att_r.at[s])

    def p_far(e):
        dst, device = (r1a, xu) if e % 2 == 0 else (r1b, xd)
        project_send(0, chunk(0), e, None, dst.at[e // 2], one_s.at[e], one_r.at[e], device)

    def p_up(e):
        extra = None
        if e % 2 == 0:
            extra = r1a.at[e // 2]
            arrived(extra, one_r.at[e])
        project_send(1, chunk(1), e, extra, r2a.at[e], two_s.at[e], two_r.at[e], xu)

    def p_down(e):
        extra = None
        if e % 2 == 1:
            extra = r1b.at[e // 2]
            arrived(extra, one_r.at[e])
        project_send(2, chunk(2), e, extra, r2b.at[e], two_s.at[8 + e], two_r.at[8 + e], xd)

    def p_mine(e):
        def put(columns, total):
            acc_ref[e, :, columns] = total

        project(chunk(3), e, None, put)

    def finish(e):
        arrived(r2a.at[e], two_r.at[e])
        arrived(r2b.at[e], two_r.at[8 + e])
        columns = pl.ds(pl.multiple_of(slots[e] * 512, 512), 512)
        out_ref[:, columns] = (
            acc_ref[e] + r2a[e].astype(jnp.float32) + r2b[e].astype(jnp.float32)
        ).astype(jnp.bfloat16)

    def attend_first(s):
        attend(chunk(s), 1 - core)
        pass_on(s)

    def attend_last(s):
        attend(chunk(s), core)

    loads[0].wait()
    z_forth(0)
    loads[1].wait()
    loads[2].wait()
    kv_own_y(1)
    z_back(0)
    pick()
    g_send()
    spread(0)
    z_forth(1)
    z_back(1)
    spread(2)
    spread(1)
    y_low(0)
    kv_own_y(0)
    kv_own_z(1)
    kv_relay_y(1)
    z_forth(2)
    spread(3)
    g_wait()
    y_high(1)
    z_back(2)
    kv_own_z(0)
    spread(4)
    kv_relay_z(1)
    g_y_send()
    y_high(3)
    y_high(0)
    kv_own_z(2)
    z_forth(3)
    kv_own_y(2)
    kv_relay_y(0)
    kv_relay_z(0)
    kv_relay2(0)
    kv_relay2(1)
    z_back(3)
    spread(5)
    y_low(3)
    y_low(1)
    y_high(4)
    kv_relay_z(2)
    z_forth(4)
    y_high(5)
    kv_relay_y(2)
    far_step(3)
    kv_own_z(3)
    y_low(2)
    g_y_wait()
    kv_wait_y(0)
    kv_wait_z(0)
    far_step(1)
    spread(6)
    far_step(0)
    kv_relay2(2)
    loads[3].wait()
    attend_first(0)
    kv_own_y(3)
    w_wait(3)
    y_low(5)
    y_high(2)
    spread(7)
    attend_last(0)
    kv_wait_y(1)
    kv_wait_z(1)
    w_wait(1)
    attend_first(1)
    w_wait(0)
    far_step(5)
    att_wait(0)
    p_far(0)
    p_far(3)
    attend_last(1)
    att_wait(1)
    kv_relay_z(3)
    kv_wait_y(2)
    kv_wait_z(2)
    p_far(1)
    far_step(2)
    y_low(4)
    p_up(1)
    y_high(6)
    attend_first(2)
    p_up(0)
    y_high(7)
    w_wait(2)
    w_wait(5)
    y_low(6)
    y_low(7)
    p_far(5)
    p_far(2)
    attend_last(2)
    kv_relay_y(3)
    far_step(4)
    att_wait(2)
    p_down(3)
    p_down(2)
    p_up(3)
    kv_relay2(3)
    w_wait(4)
    far_step(6)
    p_far(4)
    p_down(5)
    far_step(7)
    p_up(2)
    w_wait(7)
    kv_wait_y(3)
    w_wait(6)
    p_down(4)
    kv_wait_z(3)
    attend_first(3)
    p_far(7)
    p_far(6)
    p_down(6)
    p_up(4)
    att_wait(3)
    attend_last(3)
    p_down(1)
    p_up(7)
    p_up(5)
    p_mine(2)
    p_mine(3)
    finish(3)
    p_mine(0)
    p_mine(1)
    p_mine(6)
    p_up(6)
    p_mine(4)
    p_down(7)
    p_down(0)
    settle(10)
    finish(2)
    finish(1)
    p_mine(7)
    p_mine(5)
    finish(4)
    finish(5)
    finish(6)
    finish(7)
    finish(0)
    settle(0)


def shards(queries, keys, values, pairs, positions, w_out):
    bf16, f32 = jnp.bfloat16, jnp.float32
    dma = pltpu.SemaphoreType.DMA
    hbm = pl.BlockSpec(memory_space=pl.ANY)
    return pl.pallas_call(
        kernel,
        out_shape=jax.ShapeDtypeStruct((BLK, 4096), bf16),
        in_specs=[
            hbm, hbm, hbm,
            pl.BlockSpec(memory_space=pltpu.SMEM),
            pl.BlockSpec(memory_space=pltpu.VMEM),
            hbm,
        ],
        out_specs=pl.BlockSpec(memory_space=pltpu.VMEM),
        scratch_shapes=[
            pltpu.VMEM((1024, GROUPS * HD), bf16),
            pltpu.VMEM((CHUNKS, 2, ROWS, HD), bf16),
            pltpu.VMEM((5, CHUNKS, 2, ROWS, HD), bf16),
            pltpu.VMEM((2, NY, NZ * PICK, HD), bf16),
            pltpu.VMEM((NY, NZ, 512, HD), bf16),
            pltpu.VMEM((NY, NZ, 512, HD), bf16),
            pltpu.VMEM((GROUPS * BLK, KEYS), f32),
            pltpu.VMEM((GROUPS * BLK, KEYS), bf16),
            pltpu.VMEM((CHUNKS, 2, BLK, GROUPS * HD), bf16),
            pltpu.VMEM((CHUNKS, BLK, GROUPS * HD), bf16),
            pltpu.VMEM((3, 8, BLK, 512), bf16),
            pltpu.VMEM((4, BLK, 512), bf16),
            pltpu.VMEM((4, BLK, 512), bf16),
            pltpu.VMEM((8, BLK, 512), bf16),
            pltpu.VMEM((8, BLK, 512), bf16),
            pltpu.VMEM((8, BLK, 512), f32),
            pltpu.VMEM((4 * PICK, HD), f32),
            dma((4,)), dma((6, CHUNKS)), dma((5, CHUNKS)), dma((10,)), dma((10,)),
            dma((4,)), dma((4,)), dma((4,)), dma((4,)),
            dma((8,)), dma((8,)), dma((8,)), dma((8,)), dma((8,)), dma((8,)),
            dma((8,)), dma((8,)), dma((4,)), dma((4,)),
            dma((8,)), dma((8,)), dma((16,)), dma((16,)),
        ],
        compiler_params=pltpu.CompilerParams(
            collective_id=0, has_side_effects=True, vmem_limit_bytes=56 * 2**20
        ),
        name="butterfly",
    )(
        queries,
        keys.reshape(CHUNKS, ROWS, HD),
        values.reshape(CHUNKS, ROWS, HD),
        pairs,
        positions.reshape(BLOCKS, NY * NZ * PICK // BLOCKS),
        w_out,
    )


def solution(mesh):
    return jax.shard_map(
        shards,
        mesh=mesh,
        in_specs=(
            P("ctx", "head"),
            P("ctx", "head"),
            P("ctx", "head"),
            P("ctx", None),
            P(),
            P("head", "ctx"),
        ),
        out_specs=P(("ctx", "head"), None),
        check_vma=False,
    )
```

```python
import math

import jax
import jax.numpy as jnp
from jax import lax
from jax.experimental import pallas as pl
from jax.experimental.pallas import tpu as pltpu
from jax.sharding import PartitionSpec as P

HD = 128
BLK = 128
BLOCKS = 8
CHUNKS = 4
ROWS = 2 * BLK
GROUPS = 4
NY, NZ, NX = 4, 8, 4
PICK = 32
KEYS = 9 * BLK + NY * NZ * PICK
SCALE = math.log2(math.e) / math.sqrt(HD)
MESH = pl.DeviceIdType.MESH
ORDER = (2, 1, 3, 0)


def flip(value, span):
    return value + span - 2 * span * ((value // span) % 2)


def kernel(
    q_hbm, k_hbm, v_hbm, pairs_ref, pos_ref, w_hbm, out_ref,
    q_ref, kv_own, kv_in, g_ref, w_own, w_sib, s_ref, p_ref, att_ref, att_in,
    p_send, r1a, r1b, r2a, r2b, acc_ref, pick_ref,
    load_sem, kv_s, kv_r, g_ssem, g_rsem, zu_s, zu_r, zd_s, zd_r,
    yu_s, yu_r, yd_s, yd_r, far_s, far_r, sib_s, sib_r, att_s, att_r,
    one_s, one_r, two_s, two_r,
):
    ctx = lax.axis_index("ctx")
    head = lax.axis_index("head")
    z, y = ctx // NY, ctx % NY
    x, core = head // 2, head % 2

    def at(zz, yy):
        return (zz * NY + yy, head)

    z_up, z_dn = (z + 1) % NZ, (z + NZ - 1) % NZ
    y_up, y_dn, y_far = (y + 1) % NY, (y + NY - 1) % NY, (y + 2) % NY
    zu, zd, yu, yd, yf = at(z_up, y), at(z_dn, y), at(z, y_up), at(z, y_dn), at(z, y_far)
    sibling = (ctx, flip(head, 1))
    xu = (ctx, ((x + 1) % NX) * 2 + core)
    xd = (ctx, ((x + NX - 1) % NX) * 2 + core)
    z_far = (z + 4) % NZ
    z1, z2 = at(flip(z, 1), y), at(flip(z, 2), y)
    z3, z6 = at(flip(flip(z, 1), 2), y), at(flip(z_far, 2), y)
    along = [(k, (z + k) % NZ) for k in (1, 7, 2, 6, 3, 5, 4)]
    zu2, zd2 = at((z + 2) % NZ, y), at((z + 6) % NZ, y)
    y1, y3 = at(z, flip(y, 1)), at(z, flip((y + 2) % NY, 1))
    inner = ((z + 1) // 2) % 2 == 1

    loads = [
        pltpu.make_async_copy(w_hbm, w_own.at[y, z], load_sem.at[0]),
        pltpu.make_async_copy(k_hbm, kv_own.at[:, 0], load_sem.at[1]),
        pltpu.make_async_copy(v_hbm, kv_own.at[:, 1], load_sem.at[2]),
        pltpu.make_async_copy(q_hbm, q_ref, load_sem.at[3]),
    ]
    for load in loads:
        load.start()

    barrier = pltpu.get_barrier_semaphore()
    peers = [at(zz, y) for _, zz in along] + [yu, yd, yf, sibling, xu, xd]
    for peer in peers:
        pl.semaphore_signal(barrier, inc=1, device_id=peer, device_id_type=MESH)
    pl.semaphore_wait(barrier, len(peers))

    sent = []

    def send(src, dst, ssem, rsem, device, where=None):
        copy = pltpu.make_async_remote_copy(
            src_ref=src, dst_ref=dst, send_sem=ssem, recv_sem=rsem,
            device_id=device, device_id_type=MESH,
        )
        if where is None:
            copy.start()
        else:
            pl.when(where)(copy.start)
        sent.append((copy, where))

    def settle(keep):
        done = len(sent) - keep
        for copy, where in sent[:done]:
            if where is None:
                copy.wait_send()
            else:
                pl.when(where)(copy.wait_send)
        del sent[:done]

    def arrived(dst, rsem):
        pltpu.make_async_copy(dst, dst, rsem).wait()

    slots = [z, z_dn, z_up, (z + 6) % NZ, (z + 2) % NZ, (z + 5) % NZ, (z + 3) % NZ, (z + 4) % NZ]

    def spread(e):
        ref = w_own.at[y, slots[e]]
        send(ref, ref, yu_s.at[e], yu_r.at[e], yu)
        send(ref, ref, yd_s.at[e], yd_r.at[e], yd)

    def z_forth(t):
        ref = w_own.at[y, z if t == 0 else slots[2 * t - 1]]
        if t > 0:
            arrived(ref, zu_r.at[t - 1])
        if t < 4:
            send(ref, ref, zu_s.at[t], zu_r.at[t], zu)

    def z_back(t):
        ref = w_own.at[y, slots[2 * t]]
        if t > 0:
            arrived(ref, zd_r.at[t - 1])
        if t < 3:
            send(ref, ref, zd_s.at[t], zd_r.at[t], zd)

    def y_low(e):
        low = w_own.at[y_dn, slots[e]]
        arrived(low, yu_r.at[e])
        if e % 2 == 0:
            send(low, low, far_s.at[e], far_r.at[e], yu)

    def y_high(e):
        high = w_own.at[y_up, slots[e]]
        arrived(high, yd_r.at[e])
        if e % 2 == 1:
            send(high, high, far_s.at[e], far_r.at[e], yd)

    def far_step(e):
        arrived(w_own.at[y_far, slots[e]], far_r.at[e])
        send(w_own.at[:, slots[e]], w_sib.at[:, slots[e]], sib_s.at[e], sib_r.at[e], sibling)

    def chunk(s):
        return (x + ORDER[s]) % NX

    def kv_own_z(s):
        i = chunk(s)
        mine = kv_own.at[i]
        send(mine, kv_in.at[3, i], kv_s.at[1, s], kv_r.at[3, s], z2, inner)
        send(mine, kv_in.at[2, i], kv_s.at[0, s], kv_r.at[2, s], z1)

    def kv_own_y(s):
        i = chunk(s)
        send(kv_own.at[i], kv_in.at[0, i], kv_s.at[2, s], kv_r.at[0, s], y1)

    def kv_relay_z(s):
        i = chunk(s)
        near = kv_in.at[2, i]
        arrived(near, kv_r.at[2, s])
        send(near, kv_in.at[3, i], kv_s.at[3, s], kv_r.at[3, s], z3, inner)

    def kv_relay_y(s):
        i = chunk(s)
        near = kv_in.at[0, i]
        arrived(near, kv_r.at[0, s])
        send(near, kv_in.at[1, i], kv_s.at[5, s], kv_r.at[1, s], y3)

    def kv_relay2(s):
        i = chunk(s)
        mid = kv_in.at[3, i]
        arrived(mid, kv_r.at[3, s])
        send(mid, kv_in.at[4, i], kv_s.at[4, s], kv_r.at[4, s], z6)

    def kv_wait_y(s):
        arrived(kv_in.at[1, chunk(s)], kv_r.at[1, s])

    def kv_wait_z(s):
        arrived(kv_in.at[4, chunk(s)], kv_r.at[4, s])

    def pick():
        wanted = pos_ref[pl.ds(ctx // 4, 1), :]
        for part in range(2):
            picked = jnp.zeros((4 * PICK, HD), jnp.float32)
            for i in range(CHUNKS):
                spot = lax.broadcasted_iota(jnp.int32, (ROWS, 4 * PICK), 0) + (ctx * 1024 + i * ROWS)
                chosen = (spot == wanted).astype(jnp.float32).astype(jnp.bfloat16)
                picked += lax.dot_general(
                    chosen, kv_own[i, part], (((0,), (0,)), ((), ())),
                    preferred_element_type=jnp.float32,
                )
            pick_ref[...] = picked
            mine = pick_ref[pl.ds(pl.multiple_of((ctx % 4) * PICK, PICK), PICK), :]
            g_ref[part, y, pl.ds(pl.multiple_of(z * PICK, PICK), PICK), :] = mine.astype(jnp.bfloat16)

    def g_rows(zz):
        return g_ref.at[:, y, pl.ds(pl.multiple_of(zz * PICK, PICK), PICK), :]

    def g_send():
        for k, zz in along:
            send(g_rows(z), g_rows(z), g_ssem.at[2 + k], g_rsem.at[2 + k], at(zz, y))

    def g_wait():
        for k, _ in along:
            arrived(g_rows((z + NZ - k) % NZ), g_rsem.at[2 + k])

    def g_y_send():
        whole = g_ref.at[:, y]
        for n, peer in enumerate((yu, yd, yf)):
            send(whole, whole, g_ssem.at[n], g_rsem.at[n], peer)

    def g_y_wait():
        for n, yy in enumerate((y_dn, y_up, y_far)):
            arrived(g_ref.at[:, yy], g_rsem.at[n])

    def attend(i, t):
        j = 2 * i + t
        own = [j, flip(j, 1), flip(j, 2), flip(j, 4)]

        def block(part, n):
            if n < 4:
                jj = own[n]
                return kv_own[jj // 2, part, pl.ds(pl.multiple_of((jj % 2) * BLK, BLK), BLK), :]
            return kv_in[n - 4, i, part, pl.ds(pl.multiple_of(t * BLK, BLK), BLK), :]

        rows = pl.ds(pl.multiple_of(j * BLK, BLK), BLK)
        queries = jnp.concatenate(
            [q_ref[rows, h * HD : (h + 1) * HD] for h in range(GROUPS)], axis=0
        )
        contract = (((1,), (1,)), ((), ()))

        def bias(n):
            return jnp.where(pairs_ref[j, n - 1] >= 0, 0.0, -jnp.inf).astype(jnp.float32)

        for first in range(0, 9, 2):
            names = list(range(first, min(first + 2, 9)))
            keys = jnp.concatenate([block(0, n) for n in names], axis=0)
            scores = lax.dot_general(queries, keys, contract, preferred_element_type=jnp.float32)
            for m, n in enumerate(names):
                part = scores[:, m * BLK : (m + 1) * BLK]
                if n > 0:
                    part = part + bias(n)
                s_ref[:, n * BLK : (n + 1) * BLK] = part
        for yy in range(NY):
            start = 9 * BLK + yy * NZ * PICK
            s_ref[:, start : start + NZ * PICK] = lax.dot_general(
                queries, g_ref[0, yy], contract, preferred_element_type=jnp.float32
            )
        totals = []
        for r in range(0, GROUPS * BLK, 64):
            scores = s_ref[r : r + 64, :]
            top = jnp.max(scores, axis=1, keepdims=True)
            weights = jnp.exp2((scores - top) * SCALE)
            totals.append(jnp.sum(weights, axis=1, keepdims=True))
            p_ref[r : r + 64, :] = weights.astype(jnp.bfloat16)
        values = jnp.concatenate(
            [block(1, n) for n in range(9)] + [g_ref[1, yy] for yy in range(NY)], axis=0
        )
        result = jnp.dot(p_ref[...], values, preferred_element_type=jnp.float32)
        result = (result / jnp.concatenate(totals, axis=0)).astype(jnp.bfloat16)
        for h in range(GROUPS):
            att_ref[i, t, :, h * HD : (h + 1) * HD] = result[h * BLK : (h + 1) * BLK]

    def pass_on(s):
        i = chunk(s)
        send(att_ref.at[i, 1 - core], att_in.at[i], att_s.at[s], att_r.at[s], sibling)

    def project(i, e, extra, put):
        left, right = att_ref[i, core], att_in[i]
        for half in range(2):
            zz, yy = slots[e], 2 * half
            columns = slice(half * 256, half * 256 + 256)
            total = jnp.dot(
                left, jnp.concatenate([w_own[yy, zz], w_own[yy + 1, zz]], axis=1),
                preferred_element_type=jnp.float32,
            ) + jnp.dot(
                right, jnp.concatenate([w_sib[yy, zz], w_sib[yy + 1, zz]], axis=1),
                preferred_element_type=jnp.float32,
            )
            if extra is not None:
                total = total + extra[:, columns].astype(jnp.float32)
            put(columns, total)

    def project_send(n, i, e, extra, dst, ssem, rsem, device):
        def put(columns, total):
            p_send[n, e, :, columns] = total.astype(jnp.bfloat16)

        project(i, e, extra, put)
        send(p_send.at[n, e], dst, ssem, rsem, device)

    def w_wait(e):
        arrived(w_sib.at[:, slots[e]], sib_r.at[e])

    def att_wait(s):
        arrived(att_in.at[chunk(s)], att_r.at[s])

    def p_far(e):
        dst, device = (r1a, xu) if e % 2 == 0 else (r1b, xd)
        project_send(0, chunk(0), e, None, dst.at[e // 2], one_s.at[e], one_r.at[e], device)

    def p_up(e):
        extra = None
        if e % 2 == 0:
            extra = r1a.at[e // 2]
            arrived(extra, one_r.at[e])
        project_send(1, chunk(1), e, extra, r2a.at[e], two_s.at[e], two_r.at[e], xu)

    def p_down(e):
        extra = None
        if e % 2 == 1:
            extra = r1b.at[e // 2]
            arrived(extra, one_r.at[e])
        project_send(2, chunk(2), e, extra, r2b.at[e], two_s.at[8 + e], two_r.at[8 + e], xd)

    def p_mine(e):
        def put(columns, total):
            acc_ref[e, :, columns] = total

        project(chunk(3), e, None, put)

    def finish(e):
        arrived(r2a.at[e], two_r.at[e])
        arrived(r2b.at[e], two_r.at[8 + e])
        columns = pl.ds(pl.multiple_of(slots[e] * 512, 512), 512)
        out_ref[:, columns] = (
            acc_ref[e] + r2a[e].astype(jnp.float32) + r2b[e].astype(jnp.float32)
        ).astype(jnp.bfloat16)

    def attend_first(s):
        attend(chunk(s), 1 - core)
        pass_on(s)

    def attend_last(s):
        attend(chunk(s), core)

    loads[1].wait()
    loads[2].wait()
    kv_own_y(1)
    loads[0].wait()
    z_forth(0)
    pick()
    spread(0)
    z_back(0)
    kv_own_y(0)
    g_send()
    kv_relay_y(1)
    z_forth(1)
    z_back(1)
    spread(2)
    y_high(0)
    kv_own_z(0)
    spread(1)
    z_forth(2)
    g_wait()
    g_y_send()
    z_back(2)
    kv_own_y(2)
    kv_relay_z(0)
    spread(3)
    kv_relay_y(0)
    y_low(0)
    kv_own_z(1)
    kv_relay_z(1)
    y_high(1)
    y_high(2)
    z_forth(3)
    kv_own_z(2)
    kv_wait_y(1)
    z_back(3)
    spread(5)
    spread(4)
    y_high(3)
    kv_relay2(0)
    y_low(1)
    kv_relay2(1)
    far_step(0)
    kv_relay_z(2)
    z_forth(4)
    kv_wait_y(0)
    spread(6)
    g_y_wait()
    kv_relay_y(2)
    y_low(3)
    kv_own_y(3)
    kv_wait_z(0)
    far_step(1)
    y_low(2)
    loads[3].wait()
    attend_first(0)
    kv_relay2(2)
    y_high(5)
    w_wait(0)
    kv_wait_z(1)
    attend_last(0)
    far_step(3)
    attend_first(1)
    att_wait(0)
    spread(7)
    y_low(5)
    kv_own_z(3)
    attend_last(1)
    p_far(0)
    w_wait(3)
    kv_wait_y(2)
    y_low(4)
    kv_wait_z(2)
    far_step(5)
    w_wait(1)
    p_far(1)
    att_wait(1)
    p_far(3)
    far_step(2)
    p_up(3)
    y_low(6)
    attend_first(2)
    w_wait(5)
    y_high(4)
    y_high(7)
    y_low(7)
    p_far(5)
    p_up(0)
    far_step(4)
    attend_last(2)
    kv_relay_z(3)
    att_wait(2)
    y_high(6)
    p_up(1)
    w_wait(4)
    far_step(7)
    p_down(0)
    w_wait(2)
    p_down(1)
    p_down(4)
    kv_relay_y(3)
    p_far(2)
    kv_relay2(3)
    far_step(6)
    p_down(3)
    w_wait(7)
    p_far(4)
    p_up(2)
    kv_wait_y(3)
    p_down(5)
    w_wait(6)
    kv_wait_z(3)
    p_far(6)
    attend_first(3)
    p_far(7)
    p_up(4)
    attend_last(3)
    p_down(2)
    att_wait(3)
    p_mine(1)
    p_mine(0)
    p_mine(5)
    p_up(6)
    p_down(6)
    p_up(5)
    p_mine(4)
    finish(0)
    p_mine(2)
    p_mine(7)
    p_down(7)
    finish(1)
    p_up(7)
    settle(10)
    p_mine(6)
    finish(5)
    finish(6)
    p_mine(3)
    finish(4)
    finish(3)
    finish(2)
    finish(7)
    settle(0)


def shards(queries, keys, values, pairs, positions, w_out):
    bf16, f32 = jnp.bfloat16, jnp.float32
    dma = pltpu.SemaphoreType.DMA
    hbm = pl.BlockSpec(memory_space=pl.ANY)
    return pl.pallas_call(
        kernel,
        out_shape=jax.ShapeDtypeStruct((BLK, 4096), bf16),
        in_specs=[
            hbm, hbm, hbm,
            pl.BlockSpec(memory_space=pltpu.SMEM),
            pl.BlockSpec(memory_space=pltpu.VMEM),
            hbm,
        ],
        out_specs=pl.BlockSpec(memory_space=pltpu.VMEM),
        scratch_shapes=[
            pltpu.VMEM((1024, GROUPS * HD), bf16),
            pltpu.VMEM((CHUNKS, 2, ROWS, HD), bf16),
            pltpu.VMEM((5, CHUNKS, 2, ROWS, HD), bf16),
            pltpu.VMEM((2, NY, NZ * PICK, HD), bf16),
            pltpu.VMEM((NY, NZ, 512, HD), bf16),
            pltpu.VMEM((NY, NZ, 512, HD), bf16),
            pltpu.VMEM((GROUPS * BLK, KEYS), f32),
            pltpu.VMEM((GROUPS * BLK, KEYS), bf16),
            pltpu.VMEM((CHUNKS, 2, BLK, GROUPS * HD), bf16),
            pltpu.VMEM((CHUNKS, BLK, GROUPS * HD), bf16),
            pltpu.VMEM((3, 8, BLK, 512), bf16),
            pltpu.VMEM((4, BLK, 512), bf16),
            pltpu.VMEM((4, BLK, 512), bf16),
            pltpu.VMEM((8, BLK, 512), bf16),
            pltpu.VMEM((8, BLK, 512), bf16),
            pltpu.VMEM((8, BLK, 512), f32),
            pltpu.VMEM((4 * PICK, HD), f32),
            dma((4,)), dma((6, CHUNKS)), dma((5, CHUNKS)), dma((10,)), dma((10,)),
            dma((4,)), dma((4,)), dma((4,)), dma((4,)),
            dma((8,)), dma((8,)), dma((8,)), dma((8,)), dma((8,)), dma((8,)),
            dma((8,)), dma((8,)), dma((4,)), dma((4,)),
            dma((8,)), dma((8,)), dma((16,)), dma((16,)),
        ],
        compiler_params=pltpu.CompilerParams(
            collective_id=0, has_side_effects=True, vmem_limit_bytes=56 * 2**20
        ),
        name="butterfly",
    )(
        queries,
        keys.reshape(CHUNKS, ROWS, HD),
        values.reshape(CHUNKS, ROWS, HD),
        pairs,
        positions.reshape(BLOCKS, NY * NZ * PICK // BLOCKS),
        w_out,
    )


def solution(mesh):
    return jax.shard_map(
        shards,
        mesh=mesh,
        in_specs=(
            P("ctx", "head"),
            P("ctx", "head"),
            P("ctx", "head"),
            P("ctx", None),
            P(),
            P("head", "ctx"),
        ),
        out_specs=P(("ctx", "head"), None),
        check_vma=False,
    )
```
